128 devices in a mesh: fsdp: 8 (over x_hi, y), tp: 16 (over x_lo, z, core).
Axes of the slice: x: 4 (x_hi: 2, x_lo: 2; x = x_hi * 2 + x_lo), y: 4, z: 4, core: 2. Of those that a mesh axis runs over, the one named last changes fastest.
Arguments:
- tokens: bfloat16 [8192, 8192], P(('fsdp', 'tp')), may hold values from -6 to 6
- norm_gain: float32 [8192], replicated, may hold values from 0.25 to 1.75
- master_weight: float32 [8192, 26624], P(('fsdp', 'tp')), may hold values from -0.0625 to 0.0625
Outputs:
- activated: bfloat16 [8192, 26624], P('fsdp', 'tp')
The draws below stay inside these ranges and needn't reach their ends.
All inputs are finite; a program needn't handle non-finite values.
Results may differ from the reference program's by a relative error of at most 0.0058.
Values may be sent and summed in bfloat16 or wider, within the bound.
No kernel may reach another device: no remote copies, remote signals or barrier semaphores. Data moves between devices by JAX's collectives and lax.ppermute only.
A program may use at most 192 MiB of HBM per device.

```python
import jax
import jax.numpy as jnp
from jax import lax

D = 8192
FF = 26624
TOKENS = 8192


def block_scale(rng, dims, pieces, least, top_value):
    loudness, own = 1.0, jax.random.fold_in(rng, 6)
    for axis_at, shards_of in pieces:
        steps = jnp.exp(jax.random.uniform(jax.random.fold_in(own, axis_at), (shards_of,), jnp.float32, least / len(pieces), top_value / len(pieces)))
        loudness = loudness * jnp.repeat(steps, dims[axis_at] // shards_of).reshape([-1 if axis == axis_at else 1 for axis in range(len(dims))])
    return loudness


def scatter_about(rng, shape, spread, limit, shards=(), dtype=jnp.bfloat16):
    array = spread * jax.random.normal(rng, shape, jnp.float32)
    if shards:
        array = array * block_scale(rng, shape, shards, -0.22, 0.18)
    return jnp.clip(array, -limit, limit).astype(dtype)


def setup_inputs(seed: int = 0) -> dict:
    streams_of = jax.random.split(jax.random.key(seed), 4)
    tokens = scatter_about(streams_of[0], (TOKENS, D), 1.0, 6.0, ((0, 128),))
    norm_gain = jnp.clip(1.0 + 0.15 * jax.random.normal(streams_of[1], (D,), jnp.float32), 0.25, 1.75)
    master_weight = scatter_about(streams_of[2], (D, FF), D ** -0.5, 0.0625, ((0, 128),), jnp.float32)
    return {"tokens": tokens, "norm_gain": norm_gain, "master_weight": master_weight}


def reference(tokens, norm_gain, master_weight):
    wide = tokens.astype(jnp.float32)
    scale = jax.lax.rsqrt(lax.optimization_barrier(jnp.mean(wide * wide, axis=1, keepdims=True)) + 1e-05)
    normed = (wide * scale * norm_gain[None, :]).astype(jnp.bfloat16)
    serving = master_weight.astype(jnp.bfloat16)
    gate = jnp.dot(normed, serving, preferred_element_type=jnp.float32)
    return jax.nn.silu(gate).astype(jnp.bfloat16)
```

```python
import jax
import jax.numpy as jnp
from jax import lax
from jax.sharding import Mesh
from jax.sharding import PartitionSpec as P

TP = ("xl", "z", "c")
ALL = ("xh", "y", "xl", "z", "c")
CHUNKS = (384, 512, 512, 256)


def ring(size, step):
    return [(i, (i + step) % size) for i in range(size)]


def swap(x):
    return lax.ppermute(x, "xh", ring(2, 1))


def gather_y(own):
    half = own.shape[0] // 2
    right = lax.ppermute(own, "y", ring(4, 3))
    left = lax.ppermute(own, "y", ring(4, 1))
    far_top = lax.ppermute(right[:half], "y", ring(4, 3))
    far_low = lax.ppermute(left[half:], "y", ring(4, 1))
    return jnp.concatenate([own, right, far_top, far_low, left], axis=0)


def on_device(tokens, norm_gain, master_weight):
    xh, y = lax.axis_index("xh"), lax.axis_index("y")
    rows, feats = tokens.shape
    wide = tokens.astype(jnp.float32)
    scale = lax.rsqrt(jnp.mean(wide * wide, axis=1, keepdims=True) + 1e-05)
    normed = (wide * scale * norm_gain[None, :]).astype(jnp.bfloat16)
    halves = normed.reshape(rows, 2, 4, feats // 8)
    twice = jnp.concatenate([halves, halves], axis=2)
    rolled = lax.dynamic_slice_in_dim(twice, y, 4, axis=2).reshape(rows, 2, feats // 2)
    mine = lax.dynamic_index_in_dim(rolled, xh, 1, keepdims=False)
    theirs = swap(lax.dynamic_index_in_dim(rolled, 1 - xh, 1, keepdims=False))
    theirs = lax.all_gather(theirs, TP, axis=0, tiled=True)
    mine = lax.all_gather(mine, TP, axis=0, tiled=True)

    cols = master_weight.shape[1] // 16
    serving = master_weight.astype(jnp.bfloat16).reshape(rows, 16, cols)
    outs, at = [], 0
    for width in CHUNKS:
        part = serving[:, :, at : at + width]
        at += width
        own = lax.all_to_all(part, TP, split_axis=1, concat_axis=0, tiled=True)
        w = gather_y(own.reshape(rows * 16, width))
        away = jnp.dot(theirs, w, preferred_element_type=jnp.float32)
        other = swap(away.astype(jnp.bfloat16))
        gate = jnp.dot(mine, w, preferred_element_type=jnp.float32)
        outs.append(jax.nn.silu(gate + other.astype(jnp.float32)).astype(jnp.bfloat16))
    return jnp.concatenate(outs, axis=1)


def solution(mesh):
    wide = Mesh(mesh.devices.reshape(2, 4, 2, 4, 2), ALL)
    return jax.shard_map(
        on_device,
        mesh=wide,
        in_specs=(P(ALL, None), P(), P(ALL, None)),
        out_specs=P(("xh", "y"), TP),
        check_vma=False,
    )
```

```python
import functools

import jax
import jax.numpy as jnp
from jax import lax
from jax.experimental import pallas as pl
from jax.experimental.pallas import tpu as pltpu
from jax.sharding import Mesh
from jax.sharding import PartitionSpec as P

TP = ("xl", "z", "c")
ALL = ("xh", "y", "xl", "z", "c")
CHUNKS = (384, 512, 512, 256)
BF = jnp.bfloat16
F32 = jnp.float32
VMEM = 48 * 2**20
GROUPS = 4
ANY = pl.BlockSpec(memory_space=pl.ANY)


def ring(size, step):
    return [(i, (i + step) % size) for i in range(size)]


def swap(x, axis):
    return lax.ppermute(x, axis, ring(2, 1))


def cut_kernel(at, weight, *refs):
    out, wide, sems = refs[-3:]
    blocks, rows, width = wide.shape
    cols = weight.shape[1] // blocks
    copies = [
        pltpu.make_async_copy(weight.at[:, pl.ds(n * cols + at, width)], wide.at[n], sems.at[n])
        for n in range(blocks)
    ]
    for copy in copies:
        copy.start()
    for n, copy in enumerate(copies):
        copy.wait()
        out[n * rows : (n + 1) * rows, :] = wide[n].astype(BF)


def cut(weight, at, width, deps):
    rows = weight.shape[0]
    return pl.pallas_call(
        functools.partial(cut_kernel, at),
        in_specs=[ANY] * (1 + len(deps)),
        out_shape=jax.ShapeDtypeStruct((16 * rows, width), BF),
        scratch_shapes=[pltpu.VMEM((16, rows, width), F32), pltpu.SemaphoreType.DMA((16,))],
        name="cut",
    )(weight, *deps)


def tie_kernel(*refs):
    pass


def tie(x, *deps):
    return pl.pallas_call(
        tie_kernel,
        in_specs=[ANY] * (1 + len(deps)),
        out_specs=ANY,
        out_shape=jax.ShapeDtypeStruct(x.shape, x.dtype),
        input_output_aliases={0: 0},
        name="tie",
    )(x, *deps)


def norm_kernel(tokens, gain, mine, theirs, normed):
    half = mine.shape[1]
    wide = tokens[...].astype(F32)
    scale = lax.rsqrt(jnp.mean(wide * wide, axis=1, keepdims=True) + 1e-05)
    normed[...] = (wide * scale * gain[...]).astype(BF)
    xh = lax.axis_index("xh")
    mine[...] = normed[:, pl.ds(pl.multiple_of(xh * half, half), half)]
    theirs[...] = normed[:, pl.ds(pl.multiple_of((1 - xh) * half, half), half)]


def norm(tokens, gain):
    rows, feats = tokens.shape
    half = jax.ShapeDtypeStruct((rows, feats // 2), BF)
    return pl.pallas_call(
        norm_kernel,
        out_shape=[half, half],
        scratch_shapes=[pltpu.VMEM((rows, feats), BF)],
        name="norm",
    )(tokens, gain[None, :])


def load(which, pieces, w_ref, t, w, sems):
    rows, per = pieces[0].shape[1], len(pieces) // GROUPS
    wc = pltpu.make_async_copy(w_ref, w, sems.at[GROUPS])
    wc.start()
    copies = [
        pltpu.make_async_copy(p.at[which], t.at[pl.ds(n * rows, rows)], sems.at[n // per])
        for n, p in enumerate(pieces)
    ]
    for copy in copies:
        copy.start()

    def ready(group):
        if group == 0:
            wc.wait()
        for copy in copies[group * per : (group + 1) * per]:
            copy.wait()

    return ready


def away_kernel(*refs):
    pieces, w_ref, (out, t, w, sems) = refs[:16], refs[16], refs[-4:]
    ready = load(0, pieces, w_ref, t, w, sems)
    rows = t.shape[0] // GROUPS
    for group in range(GROUPS):
        ready(group)
        at = pl.ds(group * rows, rows)
        out[at, :] = jnp.dot(t[at, :], w[...], preferred_element_type=F32).astype(BF)


def scratch(pieces, w):
    rows, feats = pieces[0].shape[1:]
    return [
        pltpu.VMEM((16 * rows, feats), BF),
        pltpu.VMEM(w.shape, BF),
        pltpu.SemaphoreType.DMA((GROUPS + 1,)),
    ]


def away_dot(pieces, w, deps):
    rows = pieces[0].shape[1]
    return pl.pallas_call(
        away_kernel,
        in_specs=[ANY] * (17 + len(deps)),
        out_shape=jax.ShapeDtypeStruct((16 * rows, w.shape[1]), BF),
        scratch_shapes=scratch(pieces, w),
        compiler_params=pltpu.CompilerParams(vmem_limit_bytes=VMEM),
        name="away",
    )(*pieces, w, *deps)


def own_kernel(at_col, *refs):
    pieces, w_ref, other_ref = refs[:16], refs[16], refs[17]
    out, token, t, w, sems, other, stage, osems = refs[-8:]
    oc = pltpu.make_async_copy(other_ref, other, osems.at[GROUPS])
    oc.start()
    ready = load(1, pieces, w_ref, t, w, sems)
    rows, block = t.shape[0] // GROUPS, pieces[0].shape[1]
    xl, z, c = (lax.axis_index(a) for a in TP)
    writes = []
    oc.wait()
    for group in range(GROUPS):
        ready(group)
        at = pl.ds(group * rows, rows)
        gate = jnp.dot(t[at, :], w[...], preferred_element_type=F32) + other[at, :].astype(F32)
        stage[at, :] = (gate / (1.0 + jnp.exp(-gate))).astype(BF)
        for n in range(group * 4, group * 4 + 4):
            cr, zr, xr = n // 8, n // 2 % 4, n % 2
            where = (lax.rem(xl + xr, 2) * 4 + lax.rem(z + zr, 4)) * 2 + lax.rem(c + cr, 2)
            copy = pltpu.make_async_copy(
                stage.at[pl.ds(n * block, block)],
                out.at[pl.ds(pl.multiple_of(where * block, block), block), pl.ds(at_col, w.shape[1])],
                osems.at[group],
            )
            copy.start()
            writes.append(copy)
    token[...] = jnp.zeros_like(token)
    for copy in writes:
        copy.wait()


def own_dot(pieces, w, other, out, at_col, cols, deps):
    rows = pieces[0].shape[1]
    ins = (*deps, *(() if out is None else (out,)))
    return pl.pallas_call(
        functools.partial(own_kernel, at_col),
        in_specs=[ANY] * (18 + len(ins)),
        out_specs=[ANY, pl.BlockSpec(memory_space=pltpu.VMEM)],
        out_shape=[jax.ShapeDtypeStruct((16 * rows, cols), BF), jax.ShapeDtypeStruct((8, 128), F32)],
        scratch_shapes=scratch(pieces, w)
        + [
            pltpu.VMEM(other.shape, BF),
            pltpu.VMEM(other.shape, BF),
            pltpu.SemaphoreType.DMA((GROUPS + 1,)),
        ],
        input_output_aliases={} if out is None else {17 + len(ins): 0},
        compiler_params=pltpu.CompilerParams(vmem_limit_bytes=VMEM),
        name="own",
    )(*pieces, w, other, *ins)


def on_device(tokens, norm_gain, master_weight):
    cols = master_weight.shape[1] // 16
    ats = [sum(CHUNKS[:n]) for n in range(len(CHUNKS))]
    ws = []

    def shuffle(part):
        return lax.all_to_all(part, TP, split_axis=0, concat_axis=0, tiled=True)

    def up(x):
        return lax.ppermute(x, "z", ring(4, 3))

    def down(x):
        return lax.ppermute(x, "z", ring(4, 1))

    mine, theirs = norm(tokens, norm_gain)
    parts = [cut(master_weight, at, width, [mine]) for at, width in zip(ats, CHUNKS)]
    def gather(x):
        return lax.all_gather(x, "y", axis=0, tiled=True)

    got = swap(theirs, "xh")
    ws = [gather(shuffle(parts[0])), gather(tie(shuffle(parts[1]), got))]
    t = jnp.stack([got, mine])
    o, tup, tdown = swap(t, "xl"), up(t), down(t)
    ws.append(gather(tie(shuffle(parts[2]), o, tup, tdown)))
    oup, odown, far = up(o), down(o), up(tup)
    ws.append(gather(tie(shuffle(parts[3]), oup, odown, far)))
    ofar = down(odown)
    here = [t, o, tup, oup, far, ofar, tdown, odown]
    pieces = here + [swap(a, "c") for a in here]

    out, others, done = None, [], []
    for n in range(len(CHUNKS) + 1):
        if n < len(CHUNKS):
            away = away_dot(pieces, ws[n], [done[n - 2]] if n > 1 else [])
            others.append(swap(away, "xh"))
        if n:
            out, token = own_dot(pieces, ws[n - 1], others[n - 1], out, ats[n - 1], cols, [away])
            done.append(token)
    return out


def solution(mesh):
    wide = Mesh(mesh.devices.reshape(2, 4, 2, 4, 2), ALL)
    return jax.shard_map(
        on_device,
        mesh=wide,
        in_specs=(P(ALL, None), P(), P(ALL, None)),
        out_specs=P(("xh", "y"), TP),
        check_vma=False,
    )
```

```python
import functools

import jax
import jax.numpy as jnp
from jax import lax
from jax.experimental import pallas as pl
from jax.experimental.pallas import tpu as pltpu
from jax.sharding import Mesh
from jax.sharding import PartitionSpec as P

TP = ("xl", "z", "c")
ALL = ("xh", "y", "xl", "z", "c")
CHUNKS = (896, 512, 256)
MOST = 512
BF = jnp.bfloat16
F32 = jnp.float32
VMEM = 28 * 2**20
GROUPS = 4
ANY = pl.BlockSpec(memory_space=pl.ANY)
HERE = pl.BlockSpec(memory_space=pltpu.VMEM)


def ring(size, step):
    return [(i, (i + step) % size) for i in range(size)]


def swap(x, axis):
    return lax.ppermute(x, axis, ring(2, 1))


def cut_kernel(at, weight, *refs):
    out, wide, sems = refs[-3:]
    blocks, rows, width = wide.shape
    cols = weight.shape[1] // blocks
    copies = [
        pltpu.make_async_copy(weight.at[:, pl.ds(n * cols + at, width)], wide.at[n], sems.at[n])
        for n in range(blocks)
    ]
    for copy in copies:
        copy.start()
    for n, copy in enumerate(copies):
        copy.wait()
        out[n * rows : (n + 1) * rows, :] = wide[n].astype(BF)


def cut(weight, at, width, deps):
    rows = weight.shape[0]
    return pl.pallas_call(
        functools.partial(cut_kernel, at),
        in_specs=[ANY] * (1 + len(deps)),
        out_shape=jax.ShapeDtypeStruct((16 * rows, width), BF),
        scratch_shapes=[pltpu.VMEM((16, rows, width), F32), pltpu.SemaphoreType.DMA((16,))],
        name="cut",
    )(weight, *deps)


def tie_kernel(*refs):
    pass


def tie(x, *deps):
    return pl.pallas_call(
        tie_kernel,
        in_specs=[ANY] * (1 + len(deps)),
        out_specs=ANY,
        out_shape=jax.ShapeDtypeStruct(x.shape, x.dtype),
        input_output_aliases={0: 0},
        name="tie",
    )(x, *deps)


def norm_kernel(tokens, gain, *refs):
    mine, theirs, normed = refs[-3:]
    half = mine.shape[1]
    wide = tokens[...].astype(F32)
    scale = lax.rsqrt(jnp.mean(wide * wide, axis=1, keepdims=True) + 1e-05)
    normed[...] = (wide * scale * gain[...]).astype(BF)
    xh = lax.axis_index("xh")
    mine[...] = normed[:, pl.ds(pl.multiple_of(xh * half, half), half)]
    theirs[...] = normed[:, pl.ds(pl.multiple_of((1 - xh) * half, half), half)]


def norm(tokens, gain, deps):
    rows, feats = tokens.shape
    half = jax.ShapeDtypeStruct((rows, feats // 2), BF)
    return pl.pallas_call(
        norm_kernel,
        in_specs=[pl.BlockSpec(memory_space=pltpu.VMEM)] * 2 + [ANY] * len(deps),
        out_shape=[half, half],
        scratch_shapes=[pltpu.VMEM((rows, feats), BF)],
        name="norm",
    )(tokens, gain[None, :], *deps)


def load(t, w_refs, w, sems):
    rows, y, first, total = t.shape[0] // GROUPS, lax.axis_index("y"), 0, w.shape[0]
    weights, spans = [], []
    for n, ref in enumerate(w_refs):
        feats = ref.shape[0]
        spans.append(pl.ds(pl.multiple_of(lax.rem(y * (total // 4) + first, total), feats), feats))
        weights.append(pltpu.make_async_copy(ref, w.at[spans[-1]], sems.at[GROUPS + n]))
        first += feats
    for copy in weights:
        copy.start()

    def products(group):
        at = pl.ds(group * rows, rows)
        for lo in range(0, w.shape[1], MOST):
            part = pl.ds(lo, min(MOST, w.shape[1] - lo))
            if group:
                out = jnp.dot(t[at, :], w[:, part], preferred_element_type=F32)
            else:
                out = 0.0
                for copy, span in zip(weights, spans):
                    if lo == 0:
                        copy.wait()
                    out += jnp.dot(t[at, span], w[span, part], preferred_element_type=F32)
            yield part, out

    return products


def away_kernel(parts, t, *refs):
    w_refs, (out, w, sems) = refs[:parts], refs[-3:]
    products = load(t, w_refs, w, sems)
    rows = t.shape[0] // GROUPS
    for group in range(GROUPS):
        for part, gate in products(group):
            out[pl.ds(group * rows, rows), part] = gate.astype(BF)


def scratch(t, width):
    return [
        pltpu.VMEM((t.shape[1], width), BF),
        pltpu.SemaphoreType.DMA((GROUPS + 5,)),
    ]


def away_dot(t, ws, deps):
    width = ws[0].shape[1]
    return pl.pallas_call(
        functools.partial(away_kernel, len(ws)),
        in_specs=[HERE] + [ANY] * (len(ws) + len(deps)),
        out_shape=jax.ShapeDtypeStruct((t.shape[0], width), BF),
        scratch_shapes=scratch(t, width),
        compiler_params=pltpu.CompilerParams(vmem_limit_bytes=VMEM),
        name="away",
    )(t, *ws, *deps)


def own_kernel(to, parts, t, *refs):
    w_refs, other_ref = refs[:parts], refs[parts]
    out, token, w, sems, other, stage, osems = refs[-7:]
    oc = pltpu.make_async_copy(other_ref, other, osems.at[GROUPS])
    products = load(t, w_refs, w, sems)
    oc.start()
    rows, block = t.shape[0] // GROUPS, t.shape[0] // 16
    writes = []
    for group in range(GROUPS):
        if group == 0:
            oc.wait()
        at = pl.ds(group * rows, rows)
        for part, gate in products(group):
            gate += other[at, part].astype(F32)
            stage[at, part] = (gate / (1.0 + jnp.exp(-gate))).astype(BF)
        for n in range(group * rows // block, (group + 1) * rows // block):
            core, deep, side = n // 2 % 2, n // 4, n % 2
            here, there = pl.ds(n * block, block), pl.ds(((side * 4 + deep) * 2 + core) * block, block)
            copy = pltpu.make_async_copy(stage.at[here], out.at[there, pl.ds(to, w.shape[1])], osems.at[group])
            copy.start()
            writes.append(copy)
    token[...] = jnp.zeros_like(token)
    for copy in writes:
        copy.wait()


def own_dot(t, ws, to, other, out, cols, deps):
    ins = (*deps, *(() if out is None else (out,)))
    return pl.pallas_call(
        functools.partial(own_kernel, to, len(ws)),
        in_specs=[HERE] + [ANY] * (1 + len(ws) + len(ins)),
        out_specs=[ANY, pl.BlockSpec(memory_space=pltpu.VMEM)],
        out_shape=[jax.ShapeDtypeStruct((t.shape[0], cols), BF), jax.ShapeDtypeStruct((8, 128), F32)],
        scratch_shapes=scratch(t, other.shape[1])
        + [
            pltpu.VMEM(other.shape, BF),
            pltpu.VMEM(other.shape, BF),
            pltpu.SemaphoreType.DMA((GROUPS + 1,)),
        ],
        input_output_aliases={} if out is None else {1 + len(ws) + len(ins): 0},
        compiler_params=pltpu.CompilerParams(vmem_limit_bytes=VMEM),
        name="own",
    )(t, *ws, other, *ins)


def on_device(tokens, norm_gain, master_weight):
    cols = master_weight.shape[1] // 16
    def shuffle(n, *deps):
        part = cut(master_weight, *((0, CHUNKS[0]), (CHUNKS[0], sum(CHUNKS[1:])))[n], deps)
        return lax.all_to_all(part, TP, split_axis=0, concat_axis=0, tiled=True)

    def near(own):
        return [own, lax.ppermute(own, "y", ring(4, 3)), lax.ppermute(own, "y", ring(4, 1))]

    def far(own, right, left):
        half = own.shape[0] // 2
        top = lax.ppermute(right[:half], "y", ring(4, 3))
        low = lax.ppermute(left[half:], "y", ring(4, 1))
        return [own, right, top, low, left]

    def gather(x):
        return lax.all_gather(x, ("z", "c"), axis=0, tiled=True)

    xl = lax.axis_index("xl")

    def pair(x):
        o = swap(x, "xl")
        return jnp.concatenate([jnp.where(xl == 0, x, o), jnp.where(xl == 0, o, x)], axis=0)

    mine, theirs = norm(tokens, norm_gain, [])
    got = swap(theirs, "xh")
    own0 = shuffle(0, mine)
    near0 = near(own0)
    theirs = gather(tie(pair(got), own0))
    own1 = shuffle(1, own0)
    ws0 = far(*near0)
    both = tie(own1, *ws0[2:4])
    own1, own2 = both[:, : CHUNKS[1]], both[:, CHUNKS[1] :]
    mine = gather(tie(pair(mine), both))
    near1 = near(own1)
    away0 = away_dot(theirs, ws0, [])
    other0 = swap(away0, "xh")
    near2 = near(tie(own2, *near1[1:], away0))
    ws1 = far(*near1)
    away1 = away_dot(theirs, ws1, [])
    other1 = swap(away1, "xh")
    ws2 = far(*near2)
    away2 = away_dot(theirs, ws2, [away1])
    other2 = swap(away2, "xh")
    out, _ = own_dot(mine, ws0, 0, other0, None, cols, [away2])
    out, _ = own_dot(mine, ws1, CHUNKS[0], other1, out, cols, [])
    out, _ = own_dot(mine, ws2, sum(CHUNKS[:2]), other2, out, cols, [])
    return out


def solution(mesh):
    wide = Mesh(mesh.devices.reshape(2, 4, 2, 4, 2), ALL)
    return jax.shard_map(
        on_device,
        mesh=wide,
        in_specs=(P(ALL, None), P(), P(ALL, None)),
        out_specs=P(("xh", "y"), TP),
        check_vma=False,
    )
```

```python
import functools

import jax
import jax.numpy as jnp
from jax import lax
from jax.experimental import pallas as pl
from jax.experimental.pallas import tpu as pltpu
from jax.sharding import Mesh
from jax.sharding import PartitionSpec as P

TP = ("xl", "z", "c")
ALL = ("xh", "y", "xl", "z", "c")
CHUNKS = (896, 512, 256)
MOST = 512
BF = jnp.bfloat16
F32 = jnp.float32
VMEM = 20 * 2**20
GROUPS = 4
ANY = pl.BlockSpec(memory_space=pltpu.HBM)
HERE = pl.BlockSpec(memory_space=pltpu.VMEM)


def ring(size, step):
    return [(i, (i + step) % size) for i in range(size)]


def swap(x, axis):
    return lax.ppermute(x, axis, ring(2, 1))


def cut_kernel(at, weight, *refs):
    out, wide, sems = refs[-3:]
    blocks, rows, width = wide.shape
    cols = weight.shape[1] // blocks
    copies = [
        pltpu.make_async_copy(weight.at[:, pl.ds(n * cols + at, width)], wide.at[n], sems.at[n])
        for n in range(blocks)
    ]
    for copy in copies:
        copy.start()
    for n, copy in enumerate(copies):
        copy.wait()
        out[n * rows : (n + 1) * rows, :] = wide[n].astype(BF)


def cut(weight, at, width, deps):
    rows = weight.shape[0]
    return pl.pallas_call(
        functools.partial(cut_kernel, at),
        in_specs=[ANY] * (1 + len(deps)),
        out_shape=jax.ShapeDtypeStruct((16 * rows, width), BF),
        scratch_shapes=[pltpu.VMEM((16, rows, width), F32), pltpu.SemaphoreType.DMA((16,))],
        name="cut",
    )(weight, *deps)


def tie_kernel(*refs):
    pass


def tie(x, *deps):
    return pl.pallas_call(
        tie_kernel,
        in_specs=[ANY] * (1 + len(deps)),
        out_specs=ANY,
        out_shape=jax.ShapeDtypeStruct(x.shape, x.dtype),
        input_output_aliases={0: 0},
        name="tie",
    )(x, *deps)


def norm_kernel(tokens, gain, *refs):
    mine, theirs, normed = refs[-3:]
    half = mine.shape[1]
    wide = tokens[...].astype(F32)
    scale = lax.rsqrt(jnp.mean(wide * wide, axis=1, keepdims=True) + 1e-05)
    normed[...] = (wide * scale * gain[...]).astype(BF)
    xh = lax.axis_index("xh")
    mine[...] = normed[:, pl.ds(pl.multiple_of(xh * half, half), half)]
    theirs[...] = normed[:, pl.ds(pl.multiple_of((1 - xh) * half, half), half)]


def norm(tokens, gain, deps):
    rows, feats = tokens.shape
    half = jax.ShapeDtypeStruct((rows, feats // 2), BF)
    return pl.pallas_call(
        norm_kernel,
        in_specs=[pl.BlockSpec(memory_space=pltpu.VMEM)] * 2 + [ANY] * len(deps),
        out_shape=[half, half],
        scratch_shapes=[pltpu.VMEM((rows, feats), BF)],
        name="norm",
    )(tokens, gain[None, :], *deps)


def products(t, w_refs, group):
    rows, feats, width = t.shape[0] // GROUPS, t.shape[1], w_refs[0].shape[1]
    at, base = pl.ds(group * rows, rows), lax.axis_index("y") * (feats // 4)
    for lo in range(0, width, MOST):
        part, out, first = pl.ds(lo, min(MOST, width - lo)), 0.0, 0
        for w in w_refs:
            span = pl.ds(pl.multiple_of(lax.rem(base + first, feats), w.shape[0]), w.shape[0])
            out += jnp.dot(t[at, span], w[:, part], preferred_element_type=F32)
            first += w.shape[0]
        yield part, out


def away_kernel(parts, t, *refs):
    w_refs, out = refs[:parts], refs[-1]
    rows = t.shape[0] // GROUPS
    for group in range(GROUPS):
        for part, gate in products(t, w_refs, group):
            out[pl.ds(group * rows, rows), part] = gate.astype(BF)


def away_dot(t, ws, deps, held=()):
    return pl.pallas_call(
        functools.partial(away_kernel, len(ws)),
        in_specs=[HERE] * (1 + len(ws) + len(held)) + [ANY] * len(deps),
        out_shape=jax.ShapeDtypeStruct((t.shape[0], ws[0].shape[1]), BF),
        compiler_params=pltpu.CompilerParams(vmem_limit_bytes=VMEM),
        name="away",
    )(t, *ws, *held, *deps)


def own_kernel(to, parts, t, *refs):
    w_refs, other = refs[:parts], refs[parts]
    out, token, stage, sems = refs[-4:]
    rows, block = t.shape[0] // GROUPS, t.shape[0] // 16
    writes = []
    for group in range(GROUPS):
        at = pl.ds(group * rows, rows)
        for part, gate in products(t, w_refs, group):
            gate += other[at, part].astype(F32)
            stage[at, part] = (gate / (1.0 + jnp.exp(-gate))).astype(BF)
        for n in range(group * rows // block, (group + 1) * rows // block):
            core, deep, side = n // 2 % 2, n // 4, n % 2
            here, there = pl.ds(n * block, block), pl.ds(((side * 4 + deep) * 2 + core) * block, block)
            copy = pltpu.make_async_copy(
                stage.at[here], out.at[there, pl.ds(to, stage.shape[1])], sems.at[group]
            )
            copy.start()
            writes.append(copy)
    token[...] = jnp.zeros_like(token)
    for copy in writes:
        copy.wait()


def own_dot(t, ws, to, other, out, cols, deps):
    ins = (*deps, *(() if out is None else (out,)))
    return pl.pallas_call(
        functools.partial(own_kernel, to, len(ws)),
        in_specs=[HERE] * (2 + len(ws)) + [ANY] * len(ins),
        out_specs=[ANY, HERE],
        out_shape=[jax.ShapeDtypeStruct((t.shape[0], cols), BF), jax.ShapeDtypeStruct((8, 128), F32)],
        scratch_shapes=[pltpu.VMEM(other.shape, BF), pltpu.SemaphoreType.DMA((GROUPS,))],
        input_output_aliases={} if out is None else {1 + len(ws) + len(ins): 0},
        compiler_params=pltpu.CompilerParams(vmem_limit_bytes=VMEM),
        name="own",
    )(t, *ws, other, *ins)


def on_device(tokens, norm_gain, master_weight):
    cols = master_weight.shape[1] // 16
    def shuffle(n, *deps):
        part = cut(master_weight, *((0, CHUNKS[0]), (CHUNKS[0], sum(CHUNKS[1:])))[n], deps)
        return lax.all_to_all(part, TP, split_axis=0, concat_axis=0, tiled=True)

    def near(own):
        return [own, lax.ppermute(own, "y", ring(4, 3)), lax.ppermute(own, "y", ring(4, 1))]

    def far(own, right, left):
        half = own.shape[0] // 2
        top = lax.ppermute(right[:half], "y", ring(4, 3))
        low = lax.ppermute(left[half:], "y", ring(4, 1))
        return [own, right, top, low, left]

    def gather(x):
        return lax.all_gather(x, ("z", "c"), axis=0, tiled=True)

    xl = lax.axis_index("xl")

    def pair(x):
        o = swap(x, "xl")
        return jnp.concatenate([jnp.where(xl == 0, x, o), jnp.where(xl == 0, o, x)], axis=0)

    mine, theirs = norm(tokens, norm_gain, [])
    got = swap(theirs, "xh")
    own0 = shuffle(0, mine)
    near0 = near(own0)
    theirs = gather(tie(pair(got), own0))
    own1 = shuffle(1, own0)
    ws0 = far(*near0)
    both = tie(own1, *ws0[2:4])
    own1, own2 = both[:, : CHUNKS[1]], both[:, CHUNKS[1] :]
    mine = gather(tie(pair(mine), both))
    near1 = near(own1)
    away0 = away_dot(theirs, ws0, [])
    other0 = swap(away0, "xh")
    near2 = near(tie(own2, *near1[1:], away0))
    ws1 = far(*near1)
    away1 = away_dot(theirs, ws1, [], [mine])
    other1 = swap(away1, "xh")
    ws2 = far(*near2)
    out, token = own_dot(mine, ws0, 0, other0, None, cols, [away1])
    away2 = away_dot(theirs, ws2, [token])
    other2 = swap(away2, "xh")
    out, _ = own_dot(mine, ws1, CHUNKS[0], other1, out, cols, [away2])
    out, _ = own_dot(mine, ws2, sum(CHUNKS[:2]), other2, out, cols, [])
    return out


def solution(mesh):
    wide = Mesh(mesh.devices.reshape(2, 4, 2, 4, 2), ALL)
    return jax.shard_map(
        on_device,
        mesh=wide,
        in_specs=(P(ALL, None), P(), P(ALL, None)),
        out_specs=P(("xh", "y"), TP),
        check_vma=False,
    )
```

```python
import functools

import jax
import jax.numpy as jnp
from jax import lax
from jax.experimental import pallas as pl
from jax.experimental.pallas import tpu as pltpu
from jax.sharding import Mesh
from jax.sharding import PartitionSpec as P

TP = ("xl", "z", "c")
ALL = ("xh", "y", "xl", "z", "c")
CHUNKS = (768, 640, 256)
MOST = 512
BF = jnp.bfloat16
F32 = jnp.float32
VMEM = 20 * 2**20
GROUPS = 4
ANY = pl.BlockSpec(memory_space=pltpu.HBM)
HERE = pl.BlockSpec(memory_space=pltpu.VMEM)


def ring(size, step):
    return [(i, (i + step) % size) for i in range(size)]


def swap(x, axis):
    return lax.ppermute(x, axis, ring(2, 1))


def cut_kernel(at, weight, *refs):
    out, wide, sems = refs[-3:]
    blocks, rows, width = wide.shape
    cols = weight.shape[1] // blocks
    copies = [
        pltpu.make_async_copy(weight.at[:, pl.ds(n * cols + at, width)], wide.at[n], sems.at[n])
        for n in range(blocks)
    ]
    for copy in copies:
        copy.start()
    for n, copy in enumerate(copies):
        copy.wait()
        out[n * rows : (n + 1) * rows, :] = wide[n].astype(BF)


def cut(weight, at, width, deps):
    rows = weight.shape[0]
    return pl.pallas_call(
        functools.partial(cut_kernel, at),
        in_specs=[ANY] * (1 + len(deps)),
        out_shape=jax.ShapeDtypeStruct((16 * rows, width), BF),
        scratch_shapes=[pltpu.VMEM((16, rows, width), F32), pltpu.SemaphoreType.DMA((16,))],
        name="cut",
    )(weight, *deps)


def tie_kernel(*refs):
    pass


def tie(x, *deps):
    return pl.pallas_call(
        tie_kernel,
        in_specs=[ANY] * (1 + len(deps)),
        out_specs=ANY,
        out_shape=jax.ShapeDtypeStruct(x.shape, x.dtype),
        input_output_aliases={0: 0},
        name="tie",
    )(x, *deps)


def norm_kernel(tokens, gain, *refs):
    mine, theirs, normed = refs[-3:]
    half = mine.shape[1]
    wide = tokens[...].astype(F32)
    scale = lax.rsqrt(jnp.mean(wide * wide, axis=1, keepdims=True) + 1e-05)
    normed[...] = (wide * scale * gain[...]).astype(BF)
    xh = lax.axis_index("xh")
    mine[...] = normed[:, pl.ds(pl.multiple_of(xh * half, half), half)]
    theirs[...] = normed[:, pl.ds(pl.multiple_of((1 - xh) * half, half), half)]


def norm(tokens, gain, deps):
    rows, feats = tokens.shape
    half = jax.ShapeDtypeStruct((rows, feats // 2), BF)
    return pl.pallas_call(
        norm_kernel,
        in_specs=[pl.BlockSpec(memory_space=pltpu.VMEM)] * 2 + [ANY] * len(deps),
        out_shape=[half, half],
        scratch_shapes=[pltpu.VMEM((rows, feats), BF)],
        name="norm",
    )(tokens, gain[None, :], *deps)


def products(t, w_refs, group):
    rows, feats, width = t.shape[0] // GROUPS, t.shape[1], w_refs[0].shape[1]
    at, base = pl.ds(group * rows, rows), lax.axis_index("y") * (feats // 4)
    for lo in range(0, width, MOST):
        part, out, first = pl.ds(lo, min(MOST, width - lo)), 0.0, 0
        for w in w_refs:
            span = pl.ds(pl.multiple_of(lax.rem(base + first, feats), w.shape[0]), w.shape[0])
            out += jnp.dot(t[at, span], w[:, part], preferred_element_type=F32)
            first += w.shape[0]
        yield part, out


def away_kernel(parts, t, *refs):
    w_refs, out = refs[:parts], refs[-1]
    rows = t.shape[0] // GROUPS
    for group in range(GROUPS):
        for part, gate in products(t, w_refs, group):
            out[pl.ds(group * rows, rows), part] = gate.astype(BF)


def away_dot(t, ws, deps, held=()):
    return pl.pallas_call(
        functools.partial(away_kernel, len(ws)),
        in_specs=[HERE] * (1 + len(ws) + len(held)) + [ANY] * len(deps),
        out_shape=jax.ShapeDtypeStruct((t.shape[0], ws[0].shape[1]), BF),
        compiler_params=pltpu.CompilerParams(vmem_limit_bytes=VMEM),
        name="away",
    )(t, *ws, *held, *deps)


def own_kernel(to, parts, t, *refs):
    w_refs, other = refs[:parts], refs[parts]
    out, token, stage, sems = refs[-4:]
    rows, block = t.shape[0] // GROUPS, t.shape[0] // 16
    writes = []
    for group in range(GROUPS):
        at = pl.ds(group * rows, rows)
        for part, gate in products(t, w_refs, group):
            gate += other[at, part].astype(F32)
            stage[at, part] = (gate / (1.0 + jnp.exp(-gate))).astype(BF)
        for n in range(group * rows // block, (group + 1) * rows // block):
            core, deep, side = n // 2 % 2, n // 4, n % 2
            here, there = pl.ds(n * block, block), pl.ds(((side * 4 + deep) * 2 + core) * block, block)
            copy = pltpu.make_async_copy(
                stage.at[here], out.at[there, pl.ds(to, stage.shape[1])], sems.at[group]
            )
            copy.start()
            writes.append(copy)
    token[...] = jnp.zeros_like(token)
    for copy in writes:
        copy.wait()


def own_dot(t, ws, to, other, out, cols, deps):
    ins = (*deps, *(() if out is None else (out,)))
    return pl.pallas_call(
        functools.partial(own_kernel, to, len(ws)),
        in_specs=[HERE] * (2 + len(ws)) + [ANY] * len(ins),
        out_specs=[ANY, HERE],
        out_shape=[jax.ShapeDtypeStruct((t.shape[0], cols), BF), jax.ShapeDtypeStruct((8, 128), F32)],
        scratch_shapes=[pltpu.VMEM(other.shape, BF), pltpu.SemaphoreType.DMA((GROUPS,))],
        input_output_aliases={} if out is None else {1 + len(ws) + len(ins): 0},
        compiler_params=pltpu.CompilerParams(vmem_limit_bytes=VMEM),
        name="own",
    )(t, *ws, other, *ins)


def on_device(tokens, norm_gain, master_weight):
    cols = master_weight.shape[1] // 16
    def shuffle(n, *deps):
        part = cut(master_weight, *((0, CHUNKS[0]), (CHUNKS[0], sum(CHUNKS[1:])))[n], deps)
        return lax.all_to_all(part, TP, split_axis=0, concat_axis=0, tiled=True)

    def near(own):
        return [own, lax.ppermute(own, "y", ring(4, 3)), lax.ppermute(own, "y", ring(4, 1))]

    def far(own, right, left):
        half = own.shape[0] // 2
        top = lax.ppermute(right[:half], "y", ring(4, 3))
        low = lax.ppermute(left[half:], "y", ring(4, 1))
        return [own, right, top, low, left]

    def gather(x):
        return lax.all_gather(x, ("z", "c"), axis=0, tiled=True)

    xl = lax.axis_index("xl")

    def pair(x):
        o = swap(x, "xl")
        return jnp.concatenate([jnp.where(xl == 0, x, o), jnp.where(xl == 0, o, x)], axis=0)

    mine, theirs = norm(tokens, norm_gain, [])
    got = swap(theirs, "xh")
    own0 = shuffle(0, mine)
    near0 = near(own0)
    theirs = gather(tie(pair(got), own0))
    own1 = shuffle(1, own0)
    ws0 = far(*near0)
    both = tie(own1, *ws0[2:4])
    own1, own2 = both[:, : CHUNKS[1]], both[:, CHUNKS[1] :]
    mine = gather(tie(pair(mine), both))
    near1 = near(own1)
    away0 = away_dot(theirs, ws0, [])
    other0 = swap(away0, "xh")
    near2 = near(tie(own2, *near1[1:], away0))
    ws1 = far(*near1)
    away1 = away_dot(theirs, ws1, [])
    other1 = swap(away1, "xh")
    ws2 = far(*near2)
    out, token = own_dot(mine, ws0, 0, other0, None, cols, [away1])
    away2 = away_dot(theirs, ws2, [token])
    other2 = swap(away2, "xh")
    out, _ = own_dot(mine, ws1, CHUNKS[0], other1, out, cols, [away2])
    out, _ = own_dot(mine, ws2, sum(CHUNKS[:2]), other2, out, cols, [])
    return out


def solution(mesh):
    wide = Mesh(mesh.devices.reshape(2, 4, 2, 4, 2), ALL)
    return jax.shard_map(
        on_device,
        mesh=wide,
        in_specs=(P(ALL, None), P(), P(ALL, None)),
        out_specs=P(("xh", "y"), TP),
        check_vma=False,
    )
```
